32 devices in a mesh: row: 8 (over z, x), col: 4 (over y, core).
Axes of the slice: x: 2, y: 2, z: 4, core: 2. Of those that a mesh axis runs over, the one named last changes fastest.
Arguments:
- points: float32 [2, 2048], P(None, 'row'), may hold values from 0 to 1, as said below
- strip_ids: int32 [2048], P('row'), may hold values from 0 to 3, as said below
- counts: int32 [8], P('row'), may hold values from 128 to 256, as said below
- mode_index: int32 [1024], P('col'), may hold values from 0 to 32767, as said below
- reflectors: float32 [2048, 512], P('row'), may hold values from -0.125 to 0.125
Outputs:
- block_out: float32 [2048, 2048], P('row', 'col')
- upper_out: float32 [128, 2048], P(None, 'col')
The draws below stay inside these ranges and needn't reach their ends.
Inputs may be any that keep to these rules, and one draw needn't show every extreme that they name: `counts`: an owner's live slots come first among its 256 slots; some owner has all 256 live. `mode_index`: the modes are distinct. `points`: every point lies in the triangle x >= 0, y >= 0, x + y <= 1. `strip_ids`: A slot of owner o has strip o * 4 // 8 or one more, at most 3.
All inputs are finite; a program needn't handle non-finite values.
Results may differ from the reference program's by a relative error of at most 0.0003.
Values sent between devices are 32-bit elements; how exact they have to be, the bound alone decides.
A program may use at most 64 MiB of HBM per device.

```python
import jax
import jax.numpy as jnp
from jax import lax

CAP = 256
REFL = 512
PANEL = 128
MODES = 32768
STRIPS = 4
ROWS = 2048
OWNERS = 8
BMODES = 1024
PANELS = 4


def strip_draw(key):
    owner_ids = jnp.arange(ROWS, dtype=jnp.int32) // CAP
    base = owner_ids * STRIPS // OWNERS
    jitter = jax.random.randint(jax.random.fold_in(key, 21), (ROWS,), 0, 2)
    return jnp.minimum(base + jitter, STRIPS - 1).astype(jnp.int32)


def draw_strip_ids(key, part):
    return strip_draw(key).astype(jnp.int32)


def draw_points(key, part):
    strips = strip_draw(key)
    unit_pair = jax.random.uniform(jax.random.fold_in(key, 22), (2, ROWS), jnp.float32)
    flipped = unit_pair[0] + unit_pair[1] > 1.0
    coord_x = jnp.where(flipped, 1.0 - unit_pair[0], unit_pair[0])
    coord_y = jnp.where(flipped, 1.0 - unit_pair[1], unit_pair[1])
    shrink_rate = 0.5
    shrink = jnp.power(jnp.float32(shrink_rate), strips.astype(jnp.float32))
    return jnp.stack([coord_x * shrink, coord_y * shrink], axis=0).astype(jnp.float32)


def draw_counts(key, part):
    key_one = jax.random.fold_in(key, 11)
    key_two = jax.random.fold_in(key, 12)
    drawn = jax.random.randint(key_one, (OWNERS,), CAP // 2, CAP + 1)
    fullest = jax.random.randint(key_two, (), 0, OWNERS)
    return jnp.where(jnp.arange(OWNERS) == fullest, CAP, drawn).astype(jnp.int32)


def draw_mode_index(key, part):
    low_count = min(8, PANEL // 2)
    low_order = jax.random.permutation(jax.random.fold_in(key, 31), low_count)
    low_modes = (low_order + 124) * 128 + 2
    shuffled = jax.random.permutation(jax.random.fold_in(key, 32), MODES)
    freq_x = shuffled // 128 - 128
    freq_y = shuffled % 128 + 1
    near_zone = jnp.logical_and(jnp.abs(freq_x) <= 8, freq_y <= 8)
    ranked = jnp.argsort(near_zone.astype(jnp.int32) * MODES + jnp.arange(MODES, dtype=jnp.int32))
    remaining = shuffled[ranked][:BMODES - low_count]
    return jnp.concatenate([low_modes.astype(jnp.int32), remaining.astype(jnp.int32)]).astype(jnp.int32)


def block_scale(own_key, extent, split, least, high):
    loudness = 1.0
    for axis_at, parts in split:
        heights = jax.random.uniform(jax.random.fold_in(jax.random.fold_in(own_key, 6), axis_at), (parts,), jnp.float32, least / len(split), high / len(split))
        loudness = loudness * jnp.repeat(jnp.exp(heights), extent[axis_at] // parts).reshape((-1,) + (1,) * (len(extent) - 1 - axis_at))
    return loudness


def centred(own_key, extent, width, limit, pieces=(), held_as=jnp.bfloat16):
    values = jax.random.normal(own_key, extent, jnp.float32) * width
    if len(pieces) > 0:
        values = block_scale(own_key, extent, pieces, -0.22, 0.18) * values
    return jnp.clip(values, min=-limit, max=limit).astype(held_as)


def setup_inputs(seed: int = 0) -> dict:
    keys = jax.random.split(jax.random.key(seed), 6)
    return {
        "points": draw_points(jax.random.fold_in(keys[5], 71), 0),
        "strip_ids": draw_strip_ids(jax.random.fold_in(keys[5], 71), 0),
        "counts": draw_counts(jax.random.fold_in(keys[5], 71), 0),
        "mode_index": draw_mode_index(jax.random.fold_in(keys[5], 71), 0),
        "reflectors": centred(keys[4], (ROWS, REFL), ROWS ** -0.5, 0.125, ((0, 8),), jnp.float32),
    }


PRECISE = lax.Precision.HIGHEST
SHIFT_RATE = 1e-06

def product(left, right):
    return jnp.dot(left, right, precision=PRECISE, preferred_element_type=jnp.float32)

def transposed_product(left, right):
    return lax.dot_general(left, right, (((0,), (0,)), ((), ())), precision=PRECISE, preferred_element_type=jnp.float32)

def cholesky_lower(gram):
    order_ids = jnp.arange(gram.shape[0], dtype=jnp.int32)

    def column_step(column, lower):
        row_now = lax.dynamic_index_in_dim(lower, column, 0, keepdims=False)
        target = lax.dynamic_index_in_dim(gram, column, 1, keepdims=False) - product(lower, row_now)
        pivot = jnp.sqrt(lax.dynamic_index_in_dim(target, column, 0, keepdims=False))
        new_column = jnp.where(order_ids >= column, target / pivot, jnp.zeros_like(target))
        return lax.dynamic_update_slice_in_dim(lower, new_column[:, None], column, 1)
    return lax.fori_loop(0, gram.shape[0], column_step, jnp.zeros_like(gram))

def lower_inverse(lower):
    order_ids = jnp.arange(lower.shape[0], dtype=jnp.int32)

    def row_step(row, inverse):
        row_now = lax.dynamic_index_in_dim(lower, row, 0, keepdims=False)
        unit_row = (order_ids == row).astype(lower.dtype)
        pivot = lax.dynamic_index_in_dim(row_now, row, 0, keepdims=False)
        new_row = (unit_row - product(row_now, inverse)) / pivot
        return lax.dynamic_update_slice_in_dim(inverse, new_row[None, :], row, 0)
    return lax.fori_loop(0, lower.shape[0], row_step, jnp.zeros_like(lower))

def assemble(points, strip_ids, live_mask, mode_index):
    freq_x = (mode_index // 128 - 128).astype(jnp.float32)
    freq_y = (mode_index % 128 + 1).astype(jnp.float32)
    phases = jnp.pi * (points[0][:, None] * freq_x[None, :] + points[1][:, None] * freq_y[None, :])
    weight = 3.0 * jnp.power(10.0, -strip_ids.astype(jnp.float32) / (STRIPS - 1)) * live_mask
    columns_all = jnp.stack([jnp.cos(phases), jnp.sin(phases)], axis=-1).reshape(phases.shape[0], -1)
    return columns_all * weight[:, None]

def reflect(gram_block, coeffs):
    upper_factor = jnp.triu(gram_block, 1) + 0.5 * jnp.diag(jnp.diagonal(gram_block))
    return product(lower_inverse(upper_factor.T), coeffs)

def orthonormalize(panel_cols):
    gram_one = transposed_product(panel_cols, panel_cols)
    shift_size = SHIFT_RATE * jnp.trace(gram_one)
    lower_one = cholesky_lower(gram_one + shift_size * jnp.eye(PANEL, dtype=gram_one.dtype))
    basis_one = product(panel_cols, lower_inverse(lower_one).T)
    gram_two = transposed_product(basis_one, basis_one)
    lower_two = cholesky_lower(gram_two)
    basis_cols = product(basis_one, lower_inverse(lower_two).T)
    return (basis_cols, lower_one.T)

def reference(points, strip_ids, counts, mode_index, reflectors):
    slot_ids = jnp.arange(ROWS, dtype=jnp.int32)
    owner_ids = slot_ids // CAP
    live_mask = (slot_ids % CAP < counts[owner_ids]).astype(jnp.float32)
    work_block = assemble(points, strip_ids, live_mask, mode_index)
    stored = reflectors * live_mask[:, None]
    for panel_step in range(PANELS):
        columns = stored[:, panel_step * PANEL:(panel_step + 1) * PANEL]
        coeffs = transposed_product(columns, work_block)
        gram_block = transposed_product(columns, columns)
        work_block = work_block - product(columns, reflect(gram_block, coeffs))
    basis_cols, factor = orthonormalize(work_block[:, :PANEL])
    tail_rows = transposed_product(basis_cols, work_block)
    remainder = work_block - product(basis_cols, tail_rows)
    norm_scale = jnp.sqrt(jnp.float32(ROWS))
    block_out = jnp.concatenate([basis_cols * norm_scale, remainder[:, PANEL:]], axis=1)
    upper_out = jnp.concatenate([factor, tail_rows[:, PANEL:]], axis=1) / norm_scale
    return (block_out, upper_out)
```

```python
import functools

import jax
import jax.numpy as jnp
from jax import lax
from jax.experimental import pallas as pl
from jax.experimental.pallas import tpu as pltpu
from jax.sharding import PartitionSpec as P

PANEL = 128
STRIPS = 4
SHIFT_RATE = 1e-06
PRECISE = lax.Precision.HIGHEST
BLOCK = 256
STEP = 16


def mm(left, right):
    return jnp.dot(left, right, precision=PRECISE, preferred_element_type=jnp.float32)


def mm_t(left, right):
    return lax.dot_general(
        left, right, (((0,), (0,)), ((), ())), precision=PRECISE, preferred_element_type=jnp.float32
    )


def mm_nt(left, right):
    return lax.dot_general(
        left, right, (((1,), (1,)), ((), ())), precision=PRECISE, preferred_element_type=jnp.float32
    )


def cos_pi(turns):
    whole = jnp.round(turns)
    part = turns - whole
    odd = whole - 2.0 * jnp.floor(whole * 0.5)
    sign = 1.0 - 2.0 * odd
    sq = part * part
    coeffs = (
        -2.58068913900140e-02, 2.35330630358893e-01, -1.33526276885459e00,
        4.05871212641677e00, -4.93480220054468e00, 1.0,
    )
    acc = jnp.full_like(sq, 1.92957430940392e-03)
    for coeff in coeffs:
        acc = acc * sq + coeff
    return acc * sign


def factor_and_invert(gram, work):
    rows = lax.broadcasted_iota(jnp.int32, (PANEL, PANEL), 0)
    cols = lax.broadcasted_iota(jnp.int32, (PANEL, PANEL), 1)
    work[:, :PANEL] = gram
    work[:, PANEL:] = jnp.where(rows == cols, 1.0, 0.0)
    row_id = lax.broadcasted_iota(jnp.int32, (STEP, PANEL), 0)
    for block in range(PANEL // STEP):
        lo = block * STEP
        left = work[lo:lo + STEP, :PANEL]
        right = work[lo:lo + STEP, PANEL:]
        spread = [
            jnp.broadcast_to(left[:, lo + e:lo + e + 1], (STEP, PANEL)) for e in range(STEP)
        ]
        for c in range(STEP):
            pivot = spread[c][c:c + 1, :]
            scale = lax.rsqrt(pivot)
            scale = scale * (1.5 - 0.5 * pivot * scale * scale)
            mult = jnp.where(row_id > c, spread[c] * scale, 0.0)
            row_left = left[c:c + 1, :] * scale
            row_right = right[c:c + 1, :] * scale
            left = jnp.where(row_id == c, row_left, left - mult * row_left)
            right = jnp.where(row_id == c, row_right, right - mult * row_right)
            for e in range(c + 1, STEP):
                spread[e] = spread[e] - mult * (spread[e][c:c + 1, :] * scale)
        work[lo:lo + STEP, :PANEL] = left
        work[lo:lo + STEP, PANEL:] = right
        if lo + STEP < PANEL:
            both = jnp.concatenate([left, right], axis=1)
            update = mm_t(left, both)
            work[lo + STEP:, :] = work[lo + STEP:, :] - update[lo + STEP:, :]


def panel_kernel(points_ref, modes_ref, panel_ref, x_ref, upper_ref, base, work, gram):
    rows = points_ref.shape[1]
    width = modes_ref.shape[1]
    blocks = rows // BLOCK
    norm = float(rows) ** 0.5
    first = lax.axis_index("col") == 0
    lane = lax.broadcasted_iota(jnp.int32, (8, PANEL), 1)
    sub = lax.broadcasted_iota(jnp.int32, (8, PANEL), 0)
    pick_weight = jnp.where(sub == 3, 1.0, 0.0) + 0.0 * lane

    gram[...] = jnp.zeros_like(gram)

    @pl.loop(0, blocks)
    def _(b):
        at = pl.ds(pl.multiple_of(b * BLOCK, BLOCK), BLOCK)
        pts = points_ref[:, at]
        weight = mm_t(pts, pick_weight)
        cols = cos_pi(mm_t(pts, panel_ref[...])) * weight
        base[at, :] = cols
        gram[...] += mm_t(cols, cols)
        for q in range(width // PANEL):
            span = slice(q * PANEL, (q + 1) * PANEL)
            x_ref[at, span] = cos_pi(mm_t(pts, modes_ref[:, span])) * weight

    ri = lax.broadcasted_iota(jnp.int32, (PANEL, PANEL), 0)
    ci = lax.broadcasted_iota(jnp.int32, (PANEL, PANEL), 1)
    total = gram[...]
    trace = jnp.sum(jnp.where(ri == ci, total, 0.0))
    factor_and_invert(total + jnp.where(ri == ci, SHIFT_RATE * trace, 0.0), work)
    upper_one = jnp.where(ri <= ci, work[:, :PANEL], 0.0)
    gram[...] = jnp.zeros_like(gram)

    @pl.loop(0, blocks)
    def _(b):
        at = pl.ds(pl.multiple_of(b * BLOCK, BLOCK), BLOCK)
        cols = mm_nt(base[at, :], work[:, PANEL:])
        base[at, :] = cols
        gram[...] += mm_t(cols, cols)

    upper_ref[:, :PANEL] = upper_one
    factor_and_invert(gram[...], work)
    upper_one = upper_ref[:, :PANEL]
    upper_ref[...] = jnp.zeros_like(upper_ref)

    @pl.loop(0, blocks)
    def _(b):
        at = pl.ds(pl.multiple_of(b * BLOCK, BLOCK), BLOCK)
        cols = mm_nt(base[at, :], work[:, PANEL:])
        base[at, :] = cols
        upper_ref[...] += mm_t(cols, x_ref[at, :])

    @pl.loop(0, blocks)
    def _(b):
        at = pl.ds(pl.multiple_of(b * BLOCK, BLOCK), BLOCK)
        cols = base[at, :]
        rest = x_ref[at, :] - mm(cols, upper_ref[...])
        x_ref[at, :PANEL] = jnp.where(first, cols * norm, rest[:, :PANEL])
        x_ref[at, PANEL:] = rest[:, PANEL:]

    upper_ref[...] = upper_ref[...] / norm
    upper_ref[:, :PANEL] = jnp.where(first, upper_one / norm, upper_ref[:, :PANEL])


def reflect_kernel(v_ref, x_ref, out_ref, gram, coeffs):
    rows, depth = v_ref.shape
    blocks = rows // BLOCK
    own_rows = out_ref.shape[0]
    panels = depth // PANEL
    gram[...] = jnp.zeros_like(gram)
    coeffs[...] = jnp.zeros_like(coeffs)

    @pl.loop(0, blocks)
    def _(b):
        at = pl.ds(pl.multiple_of(b * BLOCK, BLOCK), BLOCK)
        for k in range(panels):
            cut = slice(k * PANEL, (k + 1) * PANEL)
            part = v_ref[at, cut]
            upto = slice(0, (k + 1) * PANEL)
            gram[cut, upto] += mm_t(part, v_ref[at, upto])
            coeffs[cut, :] += mm_t(part, x_ref[at, :])

    ri = lax.broadcasted_iota(jnp.int32, (PANEL, PANEL), 0)
    ci = lax.broadcasted_iota(jnp.int32, (PANEL, PANEL), 1)
    blocks_t = []
    inverses = []
    for k in range(panels):
        cut = slice(k * PANEL, (k + 1) * PANEL)
        tri = gram[cut, cut]
        half = jnp.sum(jnp.where(ri == ci, 0.5 * tri, 0.0), axis=0, keepdims=True)
        blocks_t.append(tri)
        inverses.append(jnp.where(ri == ci, 1.0 / half, 0.0))
    size = 1
    while size < PANEL:
        mask = (
            (ri // (2 * size) == ci // (2 * size))
            & ((ri // size) % 2 == 1)
            & ((ci // size) % 2 == 0)
        )
        halfway = [mm(jnp.where(mask, t, 0.0), inv) for t, inv in zip(blocks_t, inverses)]
        inverses = [inv - mm(inv, h) for h, inv in zip(halfway, inverses)]
        size *= 2
    for k in range(panels):
        cut = slice(k * PANEL, (k + 1) * PANEL)
        right = coeffs[cut, :]
        if k:
            right = right - mm(gram[cut, :k * PANEL], coeffs[:k * PANEL, :])
        coeffs[cut, :] = mm(inverses[k], right)
    own = pl.ds(pl.multiple_of(lax.axis_index("row") * own_rows, own_rows), own_rows)
    out_ref[...] = x_ref[own, :] - mm(v_ref[own, :], coeffs[...])


def on_device(points, strip_ids, counts, mode_index, reflectors):
    own_rows = points.shape[1]
    width = 2 * mode_index.shape[0]
    rows = own_rows * lax.axis_size("row")
    depth = reflectors.shape[1]
    live = (jnp.arange(own_rows, dtype=jnp.int32) < counts[0]).astype(jnp.float32)
    stored = lax.all_gather(reflectors * live[:, None], "row", axis=0, tiled=True)
    weight = 3.0 * jnp.power(10.0, -strip_ids.astype(jnp.float32) / (STRIPS - 1)) * live
    one = jnp.ones((own_rows,), jnp.float32)
    zero = jnp.zeros((own_rows,), jnp.float32)
    pts = jnp.stack([points[0], points[1], one, weight, zero, zero, zero, zero])
    pts = lax.all_gather(pts, "row", axis=1, tiled=True)
    modes = jnp.repeat(mode_index, 2)
    column = jnp.arange(width, dtype=jnp.int32)
    blank = jnp.zeros((width,), jnp.float32)
    table = jnp.stack([
        (modes // 128 - 128).astype(jnp.float32),
        (modes % 128 + 1).astype(jnp.float32),
        -0.5 * (column % 2).astype(jnp.float32),
        blank, blank, blank, blank, blank,
    ])
    panel = lax.all_gather(table[:, :PANEL], "col", axis=0, tiled=True)[:8]
    vmem = pl.BlockSpec(memory_space=pltpu.VMEM)
    x, upper = pl.pallas_call(
        panel_kernel,
        out_shape=(
            jax.ShapeDtypeStruct((rows, width), jnp.float32),
            jax.ShapeDtypeStruct((PANEL, width), jnp.float32),
        ),
        in_specs=[vmem] * 3,
        out_specs=(vmem, vmem),
        scratch_shapes=[
            pltpu.VMEM((rows, PANEL), jnp.float32),
            pltpu.VMEM((PANEL, 2 * PANEL), jnp.float32),
            pltpu.VMEM((PANEL, PANEL), jnp.float32),
        ],
        compiler_params=pltpu.CompilerParams(vmem_limit_bytes=40 * 2**20),
        name="panel",
    )(pts, table, panel)
    out = pl.pallas_call(
        reflect_kernel,
        out_shape=jax.ShapeDtypeStruct((own_rows, width), jnp.float32),
        in_specs=[vmem] * 2,
        out_specs=vmem,
        scratch_shapes=[
            pltpu.VMEM((depth, depth), jnp.float32),
            pltpu.VMEM((depth, width), jnp.float32),
        ],
        compiler_params=pltpu.CompilerParams(vmem_limit_bytes=40 * 2**20),
        name="reflect",
    )(stored, x)
    return (out, upper)


def solution(mesh):
    return jax.shard_map(
        on_device,
        mesh=mesh,
        in_specs=(P(None, "row"), P("row"), P("row"), P("col"), P("row", None)),
        out_specs=(P("row", "col"), P(None, "col")),
        check_vma=False,
    )
```

```python
import functools

import jax
import jax.numpy as jnp
from jax import lax
from jax.experimental import pallas as pl
from jax.experimental.pallas import tpu as pltpu
from jax.sharding import PartitionSpec as P

PANEL = 128
STRIPS = 4
SHIFT_RATE = 1e-06
PRECISE = lax.Precision.HIGHEST
STEP = 16


def mm(left, right):
    return jnp.dot(left, right, precision=PRECISE, preferred_element_type=jnp.float32)


def mm_t(left, right):
    return lax.dot_general(
        left, right, (((0,), (0,)), ((), ())), precision=PRECISE, preferred_element_type=jnp.float32
    )


def mm_nt(left, right):
    return lax.dot_general(
        left, right, (((1,), (1,)), ((), ())), precision=PRECISE, preferred_element_type=jnp.float32
    )


def cos_pi(turns):
    whole = jnp.round(turns)
    part = turns - whole
    odd = whole - 2.0 * jnp.floor(whole * 0.5)
    sign = 1.0 - 2.0 * odd
    sq = part * part
    coeffs = (
        -2.58068913900140e-02, 2.35330630358893e-01, -1.33526276885459e00,
        4.05871212641677e00, -4.93480220054468e00, 1.0,
    )
    acc = jnp.full_like(sq, 1.92957430940392e-03)
    for coeff in coeffs:
        acc = acc * sq + coeff
    return acc * sign


def factor_and_invert(gram, work, between=None):
    rows = lax.broadcasted_iota(jnp.int32, (PANEL, PANEL), 0)
    cols = lax.broadcasted_iota(jnp.int32, (PANEL, PANEL), 1)
    work[:, :PANEL] = gram
    work[:, PANEL:] = jnp.where(rows == cols, 1.0, 0.0)
    row_id = lax.broadcasted_iota(jnp.int32, (STEP, PANEL), 0)
    for block in range(PANEL // STEP):
        lo = block * STEP
        if between is not None:
            between(block)
        left = work[lo:lo + STEP, :PANEL]
        right = work[lo:lo + STEP, PANEL:]
        spread = [
            jnp.broadcast_to(left[:, lo + e:lo + e + 1], (STEP, PANEL)) for e in range(STEP)
        ]
        for c in range(STEP):
            pivot = spread[c][c:c + 1, :]
            scale = lax.rsqrt(pivot)
            scale = scale * (1.5 - 0.5 * pivot * scale * scale)
            mult = jnp.where(row_id > c, spread[c] * scale, 0.0)
            row_left = left[c:c + 1, :] * scale
            row_right = right[c:c + 1, :] * scale
            left = jnp.where(row_id == c, row_left, left - mult * row_left)
            right = jnp.where(row_id == c, row_right, right - mult * row_right)
            for e in range(c + 1, STEP):
                spread[e] = spread[e] - mult * (spread[e][c:c + 1, :] * scale)
        work[lo:lo + STEP, :PANEL] = left
        work[lo:lo + STEP, PANEL:] = right
        if lo + STEP < PANEL:
            both = jnp.concatenate([left, right], axis=1)
            update = mm_t(left, both)
            work[lo + STEP:, :] = work[lo + STEP:, :] - update[lo + STEP:, :]


def kernel(
    n_row, n_col, pts_in, modes_ref, v_in, out_ref, upper_ref,
    pts_all, panel_all, v_all, x_all, base, work, gram, big_gram, coeffs,
    pts_send, pts_recv, panel_send, panel_recv,
    push_send, push_recv, side_send, side_recv, core_send, core_recv,
):
    own_rows, depth = v_in.shape
    width = modes_ref.shape[1]
    panels = depth // PANEL
    rows = n_row * own_rows
    norm = float(rows) ** 0.5
    me = lax.axis_index("row")
    col = lax.axis_index("col")
    n_side = n_col // 2
    side = col // 2
    core = col % 2
    first = col == 0
    piece = own_rows // n_col

    def row_peer(k):
        return (lax.rem(me + k, n_row), col)

    def col_peer(k):
        return (me, lax.rem(col + k, n_col))

    def side_peer(k):
        return (me, lax.rem(side + k, n_side) * 2 + core)

    core_peer = (me, side * 2 + 1 - core)

    def source(k):
        return lax.rem(me + n_row - k, n_row)

    def piece_at(row, core_id, side_id):
        at = row * own_rows + (core_id * n_side + side_id) * piece
        return pl.ds(pl.multiple_of(at, piece), piece)

    def half_at(row, core_id):
        at = row * own_rows + core_id * n_side * piece
        return pl.ds(pl.multiple_of(at, piece), n_side * piece)

    def remote(src, dst, send, recv, peer):
        return pltpu.make_async_remote_copy(
            src_ref=src, dst_ref=dst, send_sem=send, recv_sem=recv,
            device_id=peer, device_id_type=pl.DeviceIdType.MESH,
        )

    def pts_copy(k, row):
        return remote(pts_in, pts_all.at[row], pts_send.at[k], pts_recv.at[k], row_peer(k))

    def panel_copy(k, index):
        return remote(
            modes_ref.at[:, pl.ds(0, PANEL)], panel_all.at[index],
            panel_send.at[k], panel_recv.at[k], col_peer(k),
        )

    def push_copy(k, row):
        mine = (core * n_side + side) * piece
        return remote(
            v_in.at[pl.ds(pl.multiple_of(mine, piece), piece)], v_all.at[piece_at(row, core, side)],
            push_send.at[k], push_recv.at[k], row_peer(k),
        )

    def side_copy(k, j, side_id):
        at = v_all.at[piece_at(source(k), core, side_id)]
        return remote(at, at, side_send.at[k, j], side_recv.at[k, j], side_peer(j))

    def core_copy(k, core_id):
        at = v_all.at[half_at(source(k), core_id)]
        return remote(at, at, core_send.at[k], core_recv.at[k], core_peer)

    barrier = pltpu.get_barrier_semaphore()
    for k in range(1, n_row):
        pl.semaphore_signal(barrier, inc=1, device_id=row_peer(k), device_id_type=pl.DeviceIdType.MESH)
    for k in range(1, n_col):
        pl.semaphore_signal(barrier, inc=1, device_id=col_peer(k), device_id_type=pl.DeviceIdType.MESH)
    pl.semaphore_wait(barrier, n_row + n_col - 2)

    for k in range(1, n_col):
        panel_copy(k, col).start()
    for k in range(1, n_row):
        pts_copy(k, me).start()
    for k in range(1, n_row):
        push_copy(k, me).start()
    pts_all[me] = pts_in[...]
    panel_all[col] = modes_ref[:, :PANEL]
    v_all[pl.ds(pl.multiple_of(me * own_rows, own_rows), own_rows), :] = v_in[...]
    for k in range(1, n_col):
        panel_copy(k, lax.rem(col + n_col - k, n_col)).wait_recv()
    for k in range(1, n_row):
        pts_copy(k, source(k)).wait_recv()

    def forward_sides(ks):
        for k in ks:
            push_copy(k, source(k)).wait_recv()
            for j in range(1, n_side):
                side_copy(k, j, side).start()

    def forward_core(ks):
        for k in ks:
            for j in range(1, n_side):
                side_copy(k, j, lax.rem(side + n_side - j, n_side)).wait_recv()
            core_copy(k, core).start()

    slots = PANEL // STEP
    share = -(-(n_row - 1) // slots)

    def turn(action):
        return lambda b: action(range(1 + b * share, min(n_row, 1 + (b + 1) * share)))

    lane = lax.broadcasted_iota(jnp.int32, (8, PANEL), 1)
    sub = lax.broadcasted_iota(jnp.int32, (8, PANEL), 0)
    pick_weight = jnp.where(sub == 3, 1.0, 0.0) + 0.0 * lane
    pick_live = jnp.where(sub == 4, 1.0, 0.0) + 0.0 * lane

    def rows_of(b):
        return pl.ds(pl.multiple_of(b * own_rows, own_rows), own_rows)

    gram[...] = jnp.zeros_like(gram)

    @pl.loop(0, n_row)
    def _(b):
        at = rows_of(b)
        pts = pts_all[b]
        weight = mm_t(pts, pick_weight)
        cols = cos_pi(mm_t(pts, panel_all[0])) * weight
        base[at, :] = cols
        gram[...] += mm_t(cols, cols)
        for q in range(width // PANEL):
            span = slice(q * PANEL, (q + 1) * PANEL)
            x_all[at, span] = cos_pi(mm_t(pts, modes_ref[:, span])) * weight

    ri = lax.broadcasted_iota(jnp.int32, (PANEL, PANEL), 0)
    ci = lax.broadcasted_iota(jnp.int32, (PANEL, PANEL), 1)
    total = gram[...]
    trace = jnp.sum(jnp.where(ri == ci, total, 0.0))
    factor_and_invert(
        total + jnp.where(ri == ci, SHIFT_RATE * trace, 0.0), work, turn(forward_sides)
    )
    upper_ref[:, :PANEL] = jnp.where(ri <= ci, work[:, :PANEL], 0.0)
    gram[...] = jnp.zeros_like(gram)

    @pl.loop(0, n_row)
    def _(b):
        at = rows_of(b)
        cols = mm_nt(base[at, :], work[:, PANEL:])
        base[at, :] = cols
        gram[...] += mm_t(cols, cols)

    factor_and_invert(gram[...], work, turn(forward_core))
    upper_one = upper_ref[:, :PANEL]
    upper_ref[...] = jnp.zeros_like(upper_ref)

    @pl.loop(0, n_row)
    def _(b):
        at = rows_of(b)
        cols = mm_nt(base[at, :], work[:, PANEL:])
        base[at, :] = cols
        upper_ref[...] += mm_t(cols, x_all[at, :])

    for k in range(1, n_row):
        core_copy(k, 1 - core).wait_recv()

    big_gram[...] = jnp.zeros_like(big_gram)
    coeffs[...] = jnp.zeros_like(coeffs)

    @pl.loop(0, n_row)
    def _(b):
        at = rows_of(b)
        cols = base[at, :]
        rest = x_all[at, :] - mm(cols, upper_ref[...])
        x_all[at, :PANEL] = jnp.where(first, cols * norm, rest[:, :PANEL])
        x_all[at, PANEL:] = rest[:, PANEL:]
        live = mm_t(pts_all[b], pick_live)
        for k in range(panels):
            cut = slice(k * PANEL, (k + 1) * PANEL)
            upto = slice(0, (k + 1) * PANEL)
            big_gram[cut, upto] += mm_t(v_all[at, cut] * live, v_all[at, upto])

    def coefficients(b):
        at = rows_of(b)
        coeffs[...] += mm_t(v_all[at, :], x_all[at, :])

    blocks_t = []
    inverses = []
    for k in range(panels):
        cut = slice(k * PANEL, (k + 1) * PANEL)
        tri = big_gram[cut, cut]
        half = jnp.sum(jnp.where(ri == ci, 0.5 * tri, 0.0), axis=0, keepdims=True)
        blocks_t.append(tri)
        inverses.append(jnp.where(ri == ci, 1.0 / half, 0.0))
    size = 1
    done = 0
    while size < PANEL:
        mask = (
            (ri // (2 * size) == ci // (2 * size))
            & ((ri // size) % 2 == 1)
            & ((ci // size) % 2 == 0)
        )
        if done < n_row:
            coefficients(done)
            done += 1
        halfway = [mm(jnp.where(mask, t, 0.0), inv) for t, inv in zip(blocks_t, inverses)]
        inverses = [inv - mm(inv, h) for h, inv in zip(halfway, inverses)]
        size *= 2

    @pl.loop(done, n_row)
    def _(b):
        coefficients(b)

    for k in range(panels):
        cut = slice(k * PANEL, (k + 1) * PANEL)
        right = coeffs[cut, :]
        if k:
            right = right - mm(big_gram[cut, :k * PANEL], coeffs[:k * PANEL, :])
        coeffs[cut, :] = mm(inverses[k], right)
    live = mm_t(pts_in[...], pick_live)
    shift = mm(v_in[...], coeffs[...])
    at = rows_of(me)
    for q in range(width // PANEL):
        span = slice(q * PANEL, (q + 1) * PANEL)
        out_ref[:, span] = x_all[at, span] - shift[:, span] * live
    upper_ref[...] = upper_ref[...] / norm
    upper_ref[:, :PANEL] = jnp.where(first, upper_one / norm, upper_ref[:, :PANEL])

    for k in range(1, n_col):
        panel_copy(k, col).wait_send()
    for k in range(1, n_row):
        pts_copy(k, me).wait_send()
        push_copy(k, me).wait_send()
        for j in range(1, n_side):
            side_copy(k, j, side).wait_send()
        core_copy(k, core).wait_send()


def on_device(points, strip_ids, counts, mode_index, reflectors):
    own_rows = points.shape[1]
    width = 2 * mode_index.shape[0]
    n_row = lax.axis_size("row")
    n_col = lax.axis_size("col")
    rows = own_rows * n_row
    depth = reflectors.shape[1]
    live = (jnp.arange(own_rows, dtype=jnp.int32) < counts[0]).astype(jnp.float32)
    weight = 3.0 * jnp.power(10.0, -strip_ids.astype(jnp.float32) / (STRIPS - 1)) * live
    one = jnp.ones((own_rows,), jnp.float32)
    zero = jnp.zeros((own_rows,), jnp.float32)
    pts = jnp.stack([points[0], points[1], one, weight, live, zero, zero, zero])
    modes = jnp.repeat(mode_index, 2)
    column = jnp.arange(width, dtype=jnp.int32)
    blank = jnp.zeros((width,), jnp.float32)
    table = jnp.stack([
        (modes // 128 - 128).astype(jnp.float32),
        (modes % 128 + 1).astype(jnp.float32),
        -0.5 * (column % 2).astype(jnp.float32),
        blank, blank, blank, blank, blank,
    ])
    vmem = pl.BlockSpec(memory_space=pltpu.VMEM)
    dma = pltpu.SemaphoreType.DMA
    n_side = n_col // 2
    return pl.pallas_call(
        functools.partial(kernel, n_row, n_col),
        out_shape=(
            jax.ShapeDtypeStruct((own_rows, width), jnp.float32),
            jax.ShapeDtypeStruct((PANEL, width), jnp.float32),
        ),
        in_specs=[vmem] * 3,
        out_specs=(vmem, vmem),
        scratch_shapes=[
            pltpu.VMEM((n_row, 8, own_rows), jnp.float32),
            pltpu.VMEM((n_col, 8, PANEL), jnp.float32),
            pltpu.VMEM((rows, depth), jnp.float32),
            pltpu.VMEM((rows, width), jnp.float32),
            pltpu.VMEM((rows, PANEL), jnp.float32),
            pltpu.VMEM((PANEL, 2 * PANEL), jnp.float32),
            pltpu.VMEM((PANEL, PANEL), jnp.float32),
            pltpu.VMEM((depth, depth), jnp.float32),
            pltpu.VMEM((depth, width), jnp.float32),
            dma((n_row,)), dma((n_row,)), dma((n_col,)), dma((n_col,)),
            dma((n_row,)), dma((n_row,)),
            dma((n_row, n_side)), dma((n_row, n_side)),
            dma((n_row,)), dma((n_row,)),
        ],
        compiler_params=pltpu.CompilerParams(
            vmem_limit_bytes=48 * 2**20, collective_id=0, has_side_effects=True
        ),
        name="window",
    )(pts, table, reflectors)


def solution(mesh):
    return jax.shard_map(
        on_device,
        mesh=mesh,
        in_specs=(P(None, "row"), P("row"), P("row"), P("col"), P("row", None)),
        out_specs=(P("row", "col"), P(None, "col")),
        check_vma=False,
    )
```

```python
import functools

import jax
import jax.numpy as jnp
from jax import lax
from jax.experimental import pallas as pl
from jax.experimental.pallas import tpu as pltpu
from jax.sharding import PartitionSpec as P

PANEL = 128
STRIPS = 4
SHIFT_RATE = 1e-06
PRECISE = lax.Precision.HIGHEST
STEP = 16


def mm(left, right):
    return jnp.dot(left, right, precision=PRECISE, preferred_element_type=jnp.float32)


def mm_t(left, right):
    return lax.dot_general(
        left, right, (((0,), (0,)), ((), ())), precision=PRECISE, preferred_element_type=jnp.float32
    )


def halves(value):
    top = value.astype(jnp.bfloat16)
    return top, (value - top.astype(jnp.float32)).astype(jnp.bfloat16)


def three_products(left, right, dims):
    left_top, left_rest = halves(left)
    right_top, right_rest = halves(right)

    def one(a, b):
        return lax.dot_general(a, b, (dims, ((), ())), preferred_element_type=jnp.float32)

    return one(left_rest, right_top) + one(left_top, right_rest) + one(left_top, right_top)


def mm_high(left, right):
    return three_products(left, right, ((1,), (0,)))


def mm_t_high(left, right):
    return three_products(left, right, ((0,), (0,)))


def mm_nt(left, right):
    return lax.dot_general(
        left, right, (((1,), (1,)), ((), ())), precision=PRECISE, preferred_element_type=jnp.float32
    )


def cos_pi(turns):
    whole = jnp.round(turns)
    part = turns - whole
    odd = whole - 2.0 * jnp.floor(whole * 0.5)
    sign = 1.0 - 2.0 * odd
    sq = part * part
    coeffs = (
        -2.58068913900140e-02, 2.35330630358893e-01, -1.33526276885459e00,
        4.05871212641677e00, -4.93480220054468e00, 1.0,
    )
    acc = jnp.full_like(sq, 1.92957430940392e-03)
    for coeff in coeffs:
        acc = acc * sq + coeff
    return acc * sign


def factor_and_invert(gram, work, between=None):
    rows = lax.broadcasted_iota(jnp.int32, (PANEL, PANEL), 0)
    cols = lax.broadcasted_iota(jnp.int32, (PANEL, PANEL), 1)
    work[:, :PANEL] = gram
    work[:, PANEL:] = jnp.where(rows == cols, 1.0, 0.0)
    row_id = lax.broadcasted_iota(jnp.int32, (STEP, PANEL), 0)
    for block in range(PANEL // STEP):
        lo = block * STEP
        if between is not None:
            between(block)
        left = work[lo:lo + STEP, :PANEL]
        right = work[lo:lo + STEP, PANEL:]
        spread = [
            jnp.broadcast_to(left[:, lo + e:lo + e + 1], (STEP, PANEL)) for e in range(STEP)
        ]
        for c in range(STEP):
            pivot = spread[c][c:c + 1, :]
            scale = lax.rsqrt(pivot)
            scale = scale * (1.5 - 0.5 * pivot * scale * scale)
            mult = jnp.where(row_id > c, spread[c] * scale, 0.0)
            row_left = left[c:c + 1, :] * scale
            row_right = right[c:c + 1, :] * scale
            left = jnp.where(row_id == c, row_left, left - mult * row_left)
            right = jnp.where(row_id == c, row_right, right - mult * row_right)
            for e in range(c + 1, STEP):
                spread[e] = spread[e] - mult * (spread[e][c:c + 1, :] * scale)
        work[lo:lo + STEP, :PANEL] = left
        work[lo:lo + STEP, PANEL:] = right
        if lo + STEP < PANEL:
            both = jnp.concatenate([left, right], axis=1)
            update = mm_t(left, both)
            work[lo + STEP:, :] = work[lo + STEP:, :] - update[lo + STEP:, :]


def kernel(
    n_row, n_col, pts_in, modes_ref, v_in, out_ref, upper_ref,
    pts_all, panel_all, v_all, x_all, base, work, gram, big_gram, coeffs,
    pts_send, pts_recv, panel_send, panel_recv,
    push_send, push_recv, side_send, side_recv, core_send, core_recv,
):
    own_rows, depth = v_in.shape
    width = modes_ref.shape[1]
    panels = depth // PANEL
    rows = n_row * own_rows
    norm = float(rows) ** 0.5
    me = lax.axis_index("row")
    col = lax.axis_index("col")
    n_side = n_col // 2
    side = col // 2
    core = col % 2
    first = col == 0
    piece = own_rows // n_col

    def flipped(k):
        index = me
        bit = 1
        while bit < n_row:
            if k & bit:
                index = index + (1 - 2 * ((me // bit) % 2)) * bit
            bit *= 2
        return index

    def row_peer(k):
        return (flipped(k), col)

    def col_peer(k):
        return (me, lax.rem(col + k, n_col))

    def side_peer(k):
        return (me, lax.rem(side + k, n_side) * 2 + core)

    core_peer = (me, side * 2 + 1 - core)

    def source(k):
        return flipped(k)

    def piece_at(row, core_id, side_id):
        at = row * own_rows + (core_id * n_side + side_id) * piece
        return pl.ds(pl.multiple_of(at, piece), piece)

    def half_at(row, core_id):
        at = row * own_rows + core_id * n_side * piece
        return pl.ds(pl.multiple_of(at, piece), n_side * piece)

    def remote(src, dst, send, recv, peer):
        return pltpu.make_async_remote_copy(
            src_ref=src, dst_ref=dst, send_sem=send, recv_sem=recv,
            device_id=peer, device_id_type=pl.DeviceIdType.MESH,
        )

    def pts_copy(k, row):
        return remote(pts_in, pts_all.at[row], pts_send.at[k], pts_recv.at[k], row_peer(k))

    def panel_copy(k, index):
        return remote(
            modes_ref.at[:, pl.ds(0, PANEL)], panel_all.at[index],
            panel_send.at[k], panel_recv.at[k], col_peer(k),
        )

    def push_copy(k, row):
        mine = (core * n_side + side) * piece
        return remote(
            v_in.at[pl.ds(pl.multiple_of(mine, piece), piece)], v_all.at[piece_at(row, core, side)],
            push_send.at[k], push_recv.at[k], row_peer(k),
        )

    def side_copy(k, j, side_id):
        at = v_all.at[piece_at(source(k), core, side_id)]
        return remote(at, at, side_send.at[k, j], side_recv.at[k, j], side_peer(j))

    def core_copy(k, core_id):
        at = v_all.at[half_at(source(k), core_id)]
        return remote(at, at, core_send.at[k], core_recv.at[k], core_peer)

    barrier = pltpu.get_barrier_semaphore()
    for k in range(1, n_row):
        pl.semaphore_signal(barrier, inc=1, device_id=row_peer(k), device_id_type=pl.DeviceIdType.MESH)
    for k in range(1, n_col):
        pl.semaphore_signal(barrier, inc=1, device_id=col_peer(k), device_id_type=pl.DeviceIdType.MESH)
    pl.semaphore_wait(barrier, n_row + n_col - 2)

    for k in range(1, n_col):
        panel_copy(k, col).start()
    for k in range(1, n_row):
        pts_copy(k, me).start()
    for k in range(1, n_row):
        push_copy(k, me).start()
    pts_all[me] = pts_in[...]
    panel_all[col] = modes_ref[:, :PANEL]
    v_all[pl.ds(pl.multiple_of(me * own_rows, own_rows), own_rows), :] = v_in[...]
    for k in range(1, n_col):
        panel_copy(k, lax.rem(col + n_col - k, n_col)).wait_recv()
    for k in range(1, n_row):
        pts_copy(k, source(k)).wait_recv()

    def forward_sides(ks):
        for k in ks:
            push_copy(k, source(k)).wait_recv()
            for j in range(1, n_side):
                side_copy(k, j, side).start()

    def forward_core(ks):
        for k in ks:
            for j in range(1, n_side):
                side_copy(k, j, lax.rem(side + n_side - j, n_side)).wait_recv()
            core_copy(k, core).start()

    slots = PANEL // STEP
    near = list(range(1, n_row // 2))
    far = list(range(n_row // 2, n_row))

    def dealt(items, block, start):
        span = slots - start
        return [k for i, k in enumerate(items) if start + i * span // len(items) == block]

    def during_first(block):
        forward_sides(dealt(near, block, slots - 3))

    def during_second(block):
        forward_sides(dealt(far, block, 1))
        forward_core(dealt(near, block, slots - 3))

    lane = lax.broadcasted_iota(jnp.int32, (8, PANEL), 1)
    sub = lax.broadcasted_iota(jnp.int32, (8, PANEL), 0)
    pick_weight = jnp.where(sub == 3, 1.0, 0.0) + 0.0 * lane
    pick_live = jnp.where(sub == 4, 1.0, 0.0) + 0.0 * lane

    def rows_of(b):
        return pl.ds(pl.multiple_of(b * own_rows, own_rows), own_rows)

    gram[...] = jnp.zeros_like(gram)

    @pl.loop(0, n_row)
    def _(b):
        at = rows_of(b)
        pts = pts_all[b]
        weight = mm_t(pts, pick_weight)
        cols = cos_pi(mm_t(pts, panel_all[0])) * weight
        base[at, :] = cols
        gram[...] += mm_t(cols, cols)
        for q in range(width // PANEL):
            span = slice(q * PANEL, (q + 1) * PANEL)
            x_all[at, span] = cos_pi(mm_t(pts, modes_ref[:, span])) * weight

    ri = lax.broadcasted_iota(jnp.int32, (PANEL, PANEL), 0)
    ci = lax.broadcasted_iota(jnp.int32, (PANEL, PANEL), 1)
    total = gram[...]
    trace = jnp.sum(jnp.where(ri == ci, total, 0.0))
    factor_and_invert(
        total + jnp.where(ri == ci, SHIFT_RATE * trace, 0.0), work, during_first
    )
    upper_ref[:, :PANEL] = jnp.where(ri <= ci, work[:, :PANEL], 0.0)
    gram[...] = jnp.zeros_like(gram)

    @pl.loop(0, n_row)
    def _(b):
        at = rows_of(b)
        cols = mm_nt(base[at, :], work[:, PANEL:])
        base[at, :] = cols
        gram[...] += mm_t(cols, cols)

    factor_and_invert(gram[...], work, during_second)
    upper_one = upper_ref[:, :PANEL]
    upper_ref[...] = jnp.zeros_like(upper_ref)

    @pl.loop(0, n_row)
    def _(b):
        at = rows_of(b)
        cols = mm_nt(base[at, :], work[:, PANEL:])
        base[at, :] = cols
        upper_ref[...] += mm_t_high(cols, x_all[at, :])

    forward_core(far)
    big_gram[...] = jnp.zeros_like(big_gram)
    coeffs[...] = jnp.zeros_like(coeffs)

    @pl.loop(0, n_row)
    def _(b):
        at = rows_of(b)
        cols = base[at, :]
        rest = x_all[at, :] - mm_high(cols, upper_ref[...])
        x_all[at, :PANEL] = jnp.where(first, cols * norm, rest[:, :PANEL])
        x_all[at, PANEL:] = rest[:, PANEL:]

    for k in range(1, n_row):
        core_copy(k, 1 - core).wait_recv()

    @pl.loop(0, n_row)
    def _(b):
        at = rows_of(b)
        live = mm_t(pts_all[b], pick_live)
        for k in range(panels):
            cut = slice(k * PANEL, (k + 1) * PANEL)
            upto = slice(0, (k + 1) * PANEL)
            big_gram[cut, upto] += mm_t_high(v_all[at, cut] * live, v_all[at, upto])

    def coefficients(b):
        at = rows_of(b)
        coeffs[...] += mm_t_high(v_all[at, :], x_all[at, :])

    blocks_t = []
    inverses = []
    for k in range(panels):
        cut = slice(k * PANEL, (k + 1) * PANEL)
        tri = big_gram[cut, cut]
        half = jnp.sum(jnp.where(ri == ci, 0.5 * tri, 0.0), axis=0, keepdims=True)
        blocks_t.append(tri)
        inverses.append(jnp.where(ri == ci, 1.0 / half, 0.0))
    size = 1
    done = 0
    while size < PANEL:
        mask = (
            (ri // (2 * size) == ci // (2 * size))
            & ((ri // size) % 2 == 1)
            & ((ci // size) % 2 == 0)
        )
        if done < n_row:
            coefficients(done)
            done += 1
        halfway = [mm(jnp.where(mask, t, 0.0), inv) for t, inv in zip(blocks_t, inverses)]
        inverses = [inv - mm(inv, h) for h, inv in zip(halfway, inverses)]
        size *= 2

    @pl.loop(done, n_row)
    def _(b):
        coefficients(b)

    for k in range(panels):
        cut = slice(k * PANEL, (k + 1) * PANEL)
        right = coeffs[cut, :]
        if k:
            right = right - mm(big_gram[cut, :k * PANEL], coeffs[:k * PANEL, :])
        coeffs[cut, :] = mm(inverses[k], right)
    live = mm_t(pts_in[...], pick_live)
    shift = mm_high(v_in[...], coeffs[...])
    at = rows_of(me)
    for q in range(width // PANEL):
        span = slice(q * PANEL, (q + 1) * PANEL)
        out_ref[:, span] = x_all[at, span] - shift[:, span] * live
    upper_ref[...] = upper_ref[...] / norm
    upper_ref[:, :PANEL] = jnp.where(first, upper_one / norm, upper_ref[:, :PANEL])

    for k in range(1, n_col):
        panel_copy(k, col).wait_send()
    for k in range(1, n_row):
        pts_copy(k, me).wait_send()
        push_copy(k, me).wait_send()
        for j in range(1, n_side):
            side_copy(k, j, side).wait_send()
        core_copy(k, core).wait_send()


def on_device(points, strip_ids, counts, mode_index, reflectors):
    own_rows = points.shape[1]
    width = 2 * mode_index.shape[0]
    n_row = lax.axis_size("row")
    n_col = lax.axis_size("col")
    rows = own_rows * n_row
    depth = reflectors.shape[1]
    live = (jnp.arange(own_rows, dtype=jnp.int32) < counts[0]).astype(jnp.float32)
    weight = 3.0 * jnp.power(10.0, -strip_ids.astype(jnp.float32) / (STRIPS - 1)) * live
    one = jnp.ones((own_rows,), jnp.float32)
    zero = jnp.zeros((own_rows,), jnp.float32)
    pts = jnp.stack([points[0], points[1], one, weight, live, zero, zero, zero])
    modes = jnp.repeat(mode_index, 2)
    column = jnp.arange(width, dtype=jnp.int32)
    blank = jnp.zeros((width,), jnp.float32)
    table = jnp.stack([
        (modes // 128 - 128).astype(jnp.float32),
        (modes % 128 + 1).astype(jnp.float32),
        -0.5 * (column % 2).astype(jnp.float32),
        blank, blank, blank, blank, blank,
    ])
    vmem = pl.BlockSpec(memory_space=pltpu.VMEM)
    dma = pltpu.SemaphoreType.DMA
    n_side = n_col // 2
    return pl.pallas_call(
        functools.partial(kernel, n_row, n_col),
        out_shape=(
            jax.ShapeDtypeStruct((own_rows, width), jnp.float32),
            jax.ShapeDtypeStruct((PANEL, width), jnp.float32),
        ),
        in_specs=[vmem] * 3,
        out_specs=(vmem, vmem),
        scratch_shapes=[
            pltpu.VMEM((n_row, 8, own_rows), jnp.float32),
            pltpu.VMEM((n_col, 8, PANEL), jnp.float32),
            pltpu.VMEM((rows, depth), jnp.float32),
            pltpu.VMEM((rows, width), jnp.float32),
            pltpu.VMEM((rows, PANEL), jnp.float32),
            pltpu.VMEM((PANEL, 2 * PANEL), jnp.float32),
            pltpu.VMEM((PANEL, PANEL), jnp.float32),
            pltpu.VMEM((depth, depth), jnp.float32),
            pltpu.VMEM((depth, width), jnp.float32),
            dma((n_row,)), dma((n_row,)), dma((n_col,)), dma((n_col,)),
            dma((n_row,)), dma((n_row,)),
            dma((n_row, n_side)), dma((n_row, n_side)),
            dma((n_row,)), dma((n_row,)),
        ],
        compiler_params=pltpu.CompilerParams(
            vmem_limit_bytes=48 * 2**20, collective_id=0, has_side_effects=True
        ),
        name="window",
    )(pts, table, reflectors)


def solution(mesh):
    return jax.shard_map(
        on_device,
        mesh=mesh,
        in_specs=(P(None, "row"), P("row"), P("row"), P("col"), P("row", None)),
        out_specs=(P("row", "col"), P(None, "col")),
        check_vma=False,
    )
```
